256 devices in a mesh: row: 16 (over x_hi, y, core), col: 16 (over x_lo, z).
Axes of the slice: x: 4 (x_hi: 2, x_lo: 2; x = x_hi * 2 + x_lo), y: 4, z: 8, core: 2. Of those that a mesh axis runs over, the one named last changes fastest.
Arguments:
- pair_map: bfloat16 [512, 512, 128], P('row', 'col'), may hold values from -6 to 6
- token_mask: int32 [512], replicated, may hold values 0 or 1
- norm_gain: float32 [2, 128], replicated, may hold values from 0.1 to 1.9
- norm_bias: float32 [2, 128], replicated, may hold values from -3 to 3
- proj_weight: bfloat16 [2, 128, 256], replicated, may hold values from -0.5 to 0.5
- gate_weight: bfloat16 [2, 128, 256], replicated, may hold values from -0.5 to 0.5
- out_gain: float32 [2, 128], replicated, may hold values from 0.1 to 1.9
- out_bias: float32 [2, 128], replicated, may hold values from -3 to 3
- final_weight: bfloat16 [2, 128, 128], replicated, may hold values from -0.5 to 0.5
- output_gate: bfloat16 [2, 128, 128], replicated, may hold values from -0.5 to 0.5
Outputs:
- updated_pair: bfloat16 [512, 512, 128], P('row', 'col')
The draws below stay inside these ranges and needn't reach their ends.
Inputs may be any that keep to these rules, and one draw needn't show every extreme that they name: `token_mask`: 1 marks a real token, 0 a padding token.
All inputs are finite; a program needn't handle non-finite values.
Results may differ from the reference program's by a relative error of at most 0.014.
Values may be sent and summed in bfloat16 or wider, within the bound.
A program may use at most 128 MiB of HBM per device.

```python
import jax
import jax.numpy as jnp
from jax import lax

C = 128
H = 128
TOKENS = 512


def with_ends(drawn, stream_key, smallest, high):
    dims = drawn.shape
    place = [jax.random.randint(jax.random.fold_in(stream_key, axis), (), 0, dims[axis]) for axis in range(len(dims))]
    drawn = drawn.at[tuple(place)].set(smallest)
    longest = dims.index(max(dims))
    place[longest] = (place[longest] + 1) % dims[longest]
    return drawn.at[tuple(place)].set(high)


def shard_levels(key, dims, split, smallest, high):
    factor_of, own = 1.0, jax.random.fold_in(key, 6)
    for dim, shards_of in split:
        heights = jnp.exp(jax.random.uniform(jax.random.fold_in(own, dim), (shards_of,), jnp.float32, smallest / len(split), high / len(split)))
        factor_of = factor_of * jnp.repeat(heights, dims[dim] // shards_of).reshape([-1 if axis == dim else 1 for axis in range(len(dims))])
    return factor_of


def normal_values(rng, extent, spread, most, shards=(), kind=jnp.bfloat16):
    array = spread * jax.random.normal(rng, extent, jnp.float32)
    if shards:
        array = array * shard_levels(rng, extent, shards, -0.22, 0.18)
    return jnp.clip(array, -most, most).astype(kind)


def setup_inputs(seed: int = 0) -> dict:
    keys = jax.random.split(jax.random.key(seed), 11)
    return {
        "pair_map": normal_values(keys[0], (TOKENS, TOKENS, C), 1.0, 6.0, ((0, 16), (1, 16))),
        "token_mask": with_ends((jax.random.randint(keys[1], (TOKENS,), 0, 8) < 7).astype(jnp.int32), jax.random.fold_in(keys[1], 1), 0, 1),
        "norm_gain": jnp.clip(1.0 + 0.18 * jax.random.normal(keys[2], (2, C), jnp.float32), 0.1, 1.9),
        "norm_bias": normal_values(keys[3], (2, C), 0.5, 3.0, (), jnp.float32),
        "proj_weight": normal_values(keys[4], (2, C, 2 * H), C ** -0.5, 0.5),
        "gate_weight": normal_values(keys[5], (2, C, 2 * H), C ** -0.5, 0.5),
        "out_gain": jnp.clip(1.0 + 0.18 * jax.random.normal(keys[6], (2, H), jnp.float32), 0.1, 1.9),
        "out_bias": normal_values(keys[7], (2, H), 0.5, 3.0, (), jnp.float32),
        "final_weight": normal_values(keys[8], (2, H, C), H ** -0.5, 0.5),
        "output_gate": normal_values(keys[9], (2, C, C), C ** -0.5, 0.5),
    }


def normalize(values, gain_vector, bias_vector):
    average = lax.optimization_barrier(jnp.mean(values, axis=-1, keepdims=True))
    centred = values - average
    variance = lax.optimization_barrier(jnp.mean(centred * centred, axis=-1, keepdims=True))
    return centred * lax.rsqrt(variance + 1e-05) * gain_vector + bias_vector

def project(pair_map, pair_mask, norm_gain, norm_bias, proj_weight, gate_weight, output_gate, layer_id):
    normed = normalize(pair_map.astype(jnp.float32), norm_gain[layer_id], norm_bias[layer_id]).astype(jnp.bfloat16)
    projected = jnp.dot(normed, proj_weight[layer_id], preferred_element_type=jnp.float32)
    gating = jnp.dot(normed, gate_weight[layer_id], preferred_element_type=jnp.float32)
    halves = (jax.nn.sigmoid(gating) * projected * pair_mask[..., None]).astype(jnp.bfloat16)
    closing = jax.nn.sigmoid(jnp.dot(normed, output_gate[layer_id], preferred_element_type=jnp.float32))
    return (halves, closing)

def finish(pair_map, summed, closing, out_gain, out_bias, final_weight, layer_id):
    lifted = normalize(summed.astype(jnp.float32), out_gain[layer_id], out_bias[layer_id]).astype(jnp.bfloat16)
    update = closing * jnp.dot(lifted, final_weight[layer_id], preferred_element_type=jnp.float32)
    return (pair_map.astype(jnp.float32) + update).astype(jnp.bfloat16)

def reference(pair_map, token_mask, norm_gain, norm_bias, proj_weight, gate_weight, out_gain, out_bias, final_weight, output_gate):
    mask_float = token_mask.astype(jnp.float32)
    pair_mask = mask_float[:, None] * mask_float[None, :]
    halves, closing = project(pair_map, pair_mask, norm_gain, norm_bias, proj_weight, gate_weight, output_gate, 0)
    left_side = halves[..., :H].astype(jnp.float32)
    right_side = halves[..., H:].astype(jnp.float32)
    summed = jnp.einsum('ikh,jkh->ijh', left_side, right_side).astype(jnp.bfloat16)
    pair_map = finish(pair_map, summed, closing, out_gain, out_bias, final_weight, 0)
    halves, closing = project(pair_map, pair_mask, norm_gain, norm_bias, proj_weight, gate_weight, output_gate, 1)
    left_side = halves[..., :H].astype(jnp.float32)
    right_side = halves[..., H:].astype(jnp.float32)
    summed = jnp.einsum('kih,kjh->ijh', left_side, right_side).astype(jnp.bfloat16)
    return finish(pair_map, summed, closing, out_gain, out_bias, final_weight, 1)
```

```python
import jax
import jax.numpy as jnp
from jax import lax
from jax.experimental import pallas as pl
from jax.experimental.pallas import tpu as pltpu
from jax.sharding import PartitionSpec as P

MESH = pl.DeviceIdType.MESH
F32 = jnp.float32
BF16 = jnp.bfloat16


def place():
    r = lax.axis_index("row")
    c = lax.axis_index("col")
    return r // 8, (r // 2) % 4, r % 2, c // 8, c % 8


def partner(me, n):
    x_hi, y, core, x_lo, z = me
    x2 = (x_hi * 2 + x_lo + n // 32) % 4
    y2 = (y + (n // 8) % 4) % 4
    z2 = (z + n % 8) % 8
    rr = (x2 // 2) * 4 + y2
    col = (x2 % 2) * 8 + z2
    return rr * 2 + core, col, rr * 16 + col


def dot(a, b, dims):
    return lax.dot_general(a, b, (dims, ((), ())), preferred_element_type=F32)


def sigmoid(v):
    return 0.5 * jnp.tanh(0.5 * v) + 0.5


def normalize(v, gain, bias):
    average = jnp.mean(v, axis=0, keepdims=True)
    centred = v - average
    variance = jnp.mean(centred * centred, axis=0, keepdims=True)
    return centred * lax.rsqrt(variance + 1e-05) * gain + bias


def chunk_swap(v):
    lane = lax.broadcasted_iota(jnp.int32, v[0].shape, 1)
    odd = (lane // 32) % 2 == 1
    high = lane >= 64

    def pair(a, b, shift, mask):
        return jnp.where(mask, pltpu.roll(b, shift, 1), a), jnp.where(
            mask, b, pltpu.roll(a, 128 - shift, 1)
        )

    a, b = pair(v[0], v[1], 32, odd)
    c, d = pair(v[2], v[3], 32, odd)
    a, c = pair(a, c, 64, high)
    b, d = pair(b, d, 64, high)
    return a, b, c, d


def kernel(
    x_ref, mask_ref, ng_ref, nb_ref, pw_ref, gw_ref, og_ref, ob_ref, fw_ref, ow_ref,
    out_ref,
    wt, ft, gb, zt, close, half, fsend, frecv, left, right, left_in, right_in, sums, bsend, brecv, wide,
    entry, f_send, f_recv, b_send, b_recv, x_send, x_recv,
):
    me = place()
    x_hi, y, core, x_lo, z = me
    row, col = lax.axis_index("row"), lax.axis_index("col")
    chip = (x_hi * 4 + y) * 16 + x_lo * 8 + z
    other = (row + 1 - 2 * core, col)

    barrier = pltpu.get_barrier_semaphore()
    ys = [partner(me, 8 * d)[:2] for d in range(1, 4)]
    xs = [partner(me, 32 * d)[:2] for d in range(1, 4)]
    zs = [partner(me, d)[:2] for d in range(1, 8)]
    for device in [other] + zs + ys + xs:
        pl.semaphore_signal(barrier, inc=1, device_id=device, device_id_type=MESH)

    lane = lax.broadcasted_iota(jnp.int32, (8, 128), 1)
    first = lax.broadcasted_iota(jnp.int32, (8, 128), 0) + 8 * (lane // 32)
    row_mask = jnp.zeros((8, 128), jnp.int32)
    col_mask = jnp.zeros((8, 128), jnp.int32)
    for a in range(32):
        row_mask = jnp.where(first == a, mask_ref[row * 32 + a], row_mask)
        col_mask = jnp.where(lane % 32 == a, mask_ref[col * 32 + a], col_mask)
    token_mask = row_mask.astype(F32) * col_mask.astype(F32)
    for u in range(2):
        for k in range(2):
            wt[u, pl.ds(128 * k, 128)] = pw_ref[u, :, pl.ds(128 * k, 128)].T
            wt[u, pl.ds(256 + 128 * k, 128)] = gw_ref[u, :, pl.ds(128 * k, 128)].T
        wt[u, pl.ds(512, 128)] = ow_ref[u].T
        ft[u] = fw_ref[u].T
        for k, ref in enumerate((ng_ref, nb_ref, og_ref, ob_ref)):
            gb[4 * u + k] = jnp.broadcast_to(ref[pl.ds(u, 1), :], (128, 128)).T

    def project(u, s, z_s):
        normed = normalize(z_s, gb[4 * u], gb[4 * u + 1]).astype(BF16)
        product = dot(wt[u], normed, ((1,), (0,)))
        close[s] = sigmoid(product[512:])
        half[pl.ds(s, 256, stride=8), :] = (
            sigmoid(product[256:512]) * product[:256] * token_mask[s : s + 1]
        )

    def send_halves(u):
        @pl.loop(0, 128)
        def _(n):
            to_row, to_col, p = partner(me, n)
            rows = pl.multiple_of(p * 8, 8)
            fsend[u, p] = jnp.concatenate(
                [half[pl.ds(rows, 8), :], half[pl.ds(rows + 1024, 8), :]], axis=0
            ).astype(BF16)

            @pl.when(n > 0)
            def _():
                pltpu.make_async_remote_copy(
                    fsend.at[u, p], frecv.at[u, chip], f_send.at[u], f_recv.at[u],
                    device_id=(to_row, to_col), device_id_type=MESH,
                ).start()

        pltpu.make_async_copy(fsend.at[u, chip], frecv.at[u, chip], f_recv.at[u]).start()

    def whole(src, dst, send, recv):
        return pltpu.make_async_remote_copy(
            src, dst, send, recv, device_id=other, device_id_type=MESH
        )

    def arrange(u):
        whole(fsend.at[u], frecv.at[u], f_send.at[u], f_recv.at[u]).wait_recv()

        @pl.loop(0, 8)
        def _(rr):
            for t in range(2):
                for g in range(2):
                    tiles = [
                        frecv[u, rr * 16 + 2 * (4 * g + k) + t].astype(F32) for k in range(4)
                    ]
                    swapped = chunk_swap(tiles)
                    rows = pl.ds(pl.multiple_of(rr * 32, 32), 32)
                    lanes = pl.ds(128 * g, 128)
                    left[u, t, rows, lanes] = jnp.concatenate(
                        [v[:8] for v in swapped], axis=0
                    ).astype(BF16)
                    right[u, t, rows, lanes] = jnp.concatenate(
                        [v[8:] for v in swapped], axis=0
                    ).astype(BF16)

    def send_sums(u):
        @pl.loop(0, 8)
        def _(rr):
            for t in range(2):
                for g in range(2):
                    tiles = [
                        sums[t, pl.ds(pl.multiple_of(rr * 32, 32) + 8 * k, 8), pl.ds(128 * g, 128)]
                        for k in range(4)
                    ]
                    for k, tile in enumerate(chunk_swap(tiles)):
                        bsend[u, rr * 16 + 2 * (4 * g + k) + t] = tile.astype(BF16)

        @pl.loop(1, 128)
        def _(n):
            to_row, to_col, p = partner(me, n)
            pltpu.make_async_remote_copy(
                bsend.at[u, p], brecv.at[u, chip], b_send.at[u], b_recv.at[u],
                device_id=(to_row, to_col), device_id_type=MESH,
            ).start()

        pltpu.make_async_copy(bsend.at[u, chip], brecv.at[u, chip], b_recv.at[u]).start()
        whole(bsend.at[u], brecv.at[u], b_send.at[u], b_recv.at[u]).wait_recv()
        wide[...] = brecv[u].astype(F32).reshape(1024, 128)

    def finish(u, s):
        summed = wide[pl.ds(s, 128, stride=8), :]
        lifted = normalize(summed, gb[4 * u + 2], gb[4 * u + 3]).astype(BF16)
        update = close[s] * dot(ft[u], lifted, ((1,), (0,)))
        return (zt[s].astype(F32) + update).astype(BF16)

    for s in range(8):
        z_s = jnp.concatenate([x_ref[8 * k + s] for k in range(4)], axis=0).T
        zt[s] = z_s
        project(0, s, z_s.astype(F32))

    pl.semaphore_wait(barrier, 14)
    for device in ys:
        pl.semaphore_signal(entry.at[0], inc=1, device_id=device, device_id_type=MESH)
    pl.semaphore_wait(entry.at[0], 3)
    for device in xs:
        pl.semaphore_signal(entry.at[1], inc=1, device_id=device, device_id_type=MESH)
    pl.semaphore_wait(entry.at[1], 3)

    send_halves(0)
    arrange(0)
    swap = whole(right.at[0], right_in.at[0], x_send.at[0], x_recv.at[0])
    swap.start()

    def outgoing(t, operand):
        sums[t] = dot(left[0, 0], operand[0], ((1,), (1,))) + dot(
            left[0, 1], operand[1], ((1,), (1,))
        )

    outgoing(core, right.at[0])
    swap.wait_recv()
    outgoing(1 - core, right_in.at[0])
    send_sums(0)

    for s in range(8):
        z_s = finish(0, s)
        zt[s] = z_s
        project(1, s, z_s.astype(F32))

    send_halves(1)
    arrange(1)
    swap_left = whole(left.at[1, 1 - core], left_in, x_send.at[1], x_recv.at[1])
    swap_right = whole(right.at[1], right_in.at[1], x_send.at[2], x_recv.at[2])
    swap_left.start()
    swap_right.start()
    for t in range(2):
        sums[t] = dot(left[1, core], right[1, t], ((0,), (0,)))
    swap_left.wait_recv()
    swap_right.wait_recv()
    for t in range(2):
        sums[t] = sums[t] + dot(left_in[...], right_in[1, t], ((0,), (0,)))
    send_sums(1)

    for s in range(8):
        z_s = finish(1, s).T
        for k in range(4):
            out_ref[8 * k + s] = z_s[32 * k : 32 * k + 32]

    swap.wait_send()
    swap_left.wait_send()
    swap_right.wait_send()
    most = pl.ds(0, 127)
    for u in range(2):
        whole(fsend.at[u, most], frecv.at[u, most], f_send.at[u], f_recv.at[u]).wait_send()
        whole(bsend.at[u, most], brecv.at[u, most], b_send.at[u], b_recv.at[u]).wait_send()


def shards(*arrays):
    vmem = pl.BlockSpec(memory_space=pltpu.VMEM)
    smem = pl.BlockSpec(memory_space=pltpu.SMEM)
    return pl.pallas_call(
        kernel,
        out_shape=jax.ShapeDtypeStruct(arrays[0].shape, BF16),
        in_specs=[vmem, smem] + [vmem] * 8,
        out_specs=vmem,
        scratch_shapes=[
            pltpu.VMEM((2, 640, 128), BF16),
            pltpu.VMEM((2, 128, 128), BF16),
            pltpu.VMEM((8, 128, 128), F32),
            pltpu.VMEM((8, 128, 128), BF16),
            pltpu.VMEM((8, 128, 128), F32),
            pltpu.VMEM((2048, 128), F32),
            pltpu.VMEM((2, 128, 16, 128), BF16),
            pltpu.VMEM((2, 128, 16, 128), BF16),
            pltpu.VMEM((2, 2, 256, 256), BF16),
            pltpu.VMEM((2, 2, 256, 256), BF16),
            pltpu.VMEM((256, 256), BF16),
            pltpu.VMEM((2, 2, 256, 256), BF16),
            pltpu.VMEM((2, 256, 256), F32),
            pltpu.VMEM((2, 128, 8, 128), BF16),
            pltpu.VMEM((2, 128, 8, 128), BF16),
            pltpu.VMEM((1024, 128), F32),
            pltpu.SemaphoreType.REGULAR((2,)),
            pltpu.SemaphoreType.DMA((2,)),
            pltpu.SemaphoreType.DMA((2,)),
            pltpu.SemaphoreType.DMA((2,)),
            pltpu.SemaphoreType.DMA((2,)),
            pltpu.SemaphoreType.DMA((3,)),
            pltpu.SemaphoreType.DMA((3,)),
        ],
        compiler_params=pltpu.CompilerParams(
            collective_id=0, has_side_effects=True, vmem_limit_bytes=32 << 20
        ),
    )(*arrays)


def solution(mesh):
    return jax.shard_map(
        shards,
        mesh=mesh,
        in_specs=(P("row", "col", None), P(), P(), P(), P(), P(), P(), P(), P(), P()),
        out_specs=P("row", "col", None),
        check_vma=False,
    )
```

```python
import jax
import jax.numpy as jnp
from jax import lax
from jax.experimental import pallas as pl
from jax.experimental.pallas import tpu as pltpu
from jax.sharding import PartitionSpec as P

MESH = pl.DeviceIdType.MESH
F32 = jnp.float32
BF16 = jnp.bfloat16


def far_first(n):
    return n + 2 - (n // 2) * (2 * n - 1)


def dot(a, b, dims):
    return lax.dot_general(a, b, (dims, ((), ())), preferred_element_type=F32)


def sigmoid(v):
    return 0.5 * jnp.tanh(0.5 * v) + 0.5


def normalize(v, gain, bias):
    average = jnp.mean(v, axis=0, keepdims=True)
    centred = v - average
    variance = jnp.mean(centred * centred, axis=0, keepdims=True)
    return centred * lax.rsqrt(variance + 1e-05) * gain + bias


def chunk_swap(v):
    lane = lax.broadcasted_iota(jnp.int32, v[0].shape, 1)
    odd = (lane // 32) % 2 == 1
    high = lane >= 64

    def pair(a, b, shift, mask):
        return jnp.where(mask, pltpu.roll(b, shift, 1), a), jnp.where(
            mask, b, pltpu.roll(a, 128 - shift, 1)
        )

    a, b = pair(v[0], v[1], 32, odd)
    c, d = pair(v[2], v[3], 32, odd)
    a, c = pair(a, c, 64, high)
    b, d = pair(b, d, 64, high)
    return a, b, c, d


def kernel(
    x_hbm, mask_hbm, ng_hbm, nb_hbm, pw_hbm, gw_hbm, og_hbm, ob_hbm, fw_hbm, ow_hbm,
    out_ref,
    x_ref, mask_ref, ng_ref, nb_ref, pw_ref, gw_ref, og_ref, ob_ref, fw_ref, ow_ref,
    wt, ft, gb, zt, close, half, fsend, frecv, left, right, left_in, right_in, sums, bsend, brecv, wide,
    in_sem, entry, f_send, f_recv, b_send, b_recv, x_send, x_recv,
):
    row, col = lax.axis_index("row"), lax.axis_index("col")
    core = row % 2
    x, y, z = (row // 8) * 2 + col // 8, (row // 2) % 4, col % 8
    other = (row + 1 - 2 * core, col)

    hbm = (x_hbm, mask_hbm, ng_hbm, nb_hbm, pw_hbm, gw_hbm, og_hbm, ob_hbm, fw_hbm, ow_hbm)
    held = (x_ref, mask_ref, ng_ref, nb_ref, pw_ref, gw_ref, og_ref, ob_ref, fw_ref, ow_ref)
    inputs = [
        pltpu.make_async_copy(a, b, in_sem.at[k]) for k, (a, b) in enumerate(zip(hbm, held))
    ]
    for copy in inputs:
        copy.start()

    def line(x, y):
        x, y = (x + 4) % 4, (y + 4) % 4
        rr, base = (x // 2) * 4 + y, (x % 2) * 8
        return rr * 2 + core, base, rr * 16 + base

    chip = line(x, y)[2] + z
    ring = [(z + d) % 8 for d in range(8)]
    outward = (4, 3, 5, 2, 6, 1, 7, 0)

    barrier = pltpu.get_barrier_semaphore()
    for dx in (2, 1, 3):
        to_row, base, _ = line(x + dx, y)
        pl.semaphore_signal(barrier, inc=1, device_id=(to_row, base + z), device_id_type=MESH)
    for dy in (2, 1, 3, 0):
        to_row, base, _ = line(x, y + dy)
        for dz in outward[: 8 if dy else 7]:
            pl.semaphore_signal(
                barrier, inc=1, device_id=(to_row, base + ring[dz]), device_id_type=MESH
            )
    pl.semaphore_signal(barrier, inc=1, device_id=other, device_id_type=MESH)

    for copy in inputs:
        copy.wait()

    lane = lax.broadcasted_iota(jnp.int32, (8, 128), 1)
    first = lax.broadcasted_iota(jnp.int32, (8, 128), 0) + 8 * (lane // 32)
    row_mask = jnp.zeros((8, 128), jnp.int32)
    col_mask = jnp.zeros((8, 128), jnp.int32)
    for a in range(32):
        row_mask = jnp.where(first == a, mask_ref[row * 32 + a], row_mask)
        col_mask = jnp.where(lane % 32 == a, mask_ref[col * 32 + a], col_mask)
    token_mask = row_mask.astype(F32) * col_mask.astype(F32)

    def prepare(u):
        for k in range(2):
            wt[u, pl.ds(128 * k, 128)] = pw_ref[u, :, pl.ds(128 * k, 128)].T
            wt[u, pl.ds(256 + 128 * k, 128)] = gw_ref[u, :, pl.ds(128 * k, 128)].T
        wt[u, pl.ds(512, 128)] = ow_ref[u].T
        ft[u] = fw_ref[u].T
        for k, ref in enumerate((ng_ref, nb_ref, og_ref, ob_ref)):
            gb[4 * u + k] = jnp.broadcast_to(ref[pl.ds(u, 1), :], (128, 128)).T

    def project(u, s, z_s):
        normed = normalize(z_s, gb[4 * u], gb[4 * u + 1]).astype(BF16)
        product = dot(wt[u], normed, ((1,), (0,)))
        close[s] = sigmoid(product[512:])
        half[pl.ds(s, 256, stride=8), :] = (
            sigmoid(product[256:512]) * product[:256] * token_mask[s : s + 1]
        )

    def send_line(u, dx, dy, m):
        to_row, base, p = line(x + dx, y + dy)
        rows = pl.multiple_of(p * 8, 64)
        fsend[u, pl.ds(p, 8)] = jnp.concatenate(
            [
                half[pl.ds(rows, 64), :].reshape(8, 8, 128),
                half[pl.ds(rows + 1024, 64), :].reshape(8, 8, 128),
            ],
            axis=1,
        ).astype(BF16)
        for dz in outward:
            to = p + ring[dz]

            def send():
                pltpu.make_async_remote_copy(
                    fsend.at[u, to], frecv.at[u, chip], f_send.at[u], f_recv.at[u, m],
                    device_id=(to_row, base + ring[dz]), device_id_type=MESH,
                ).start()

            if dz:
                send()
            else:
                here = to == chip
                pl.when(jnp.logical_not(here))(send)

                @pl.when(here)
                def _():
                    pltpu.make_async_copy(
                        fsend.at[u, to], frecv.at[u, chip], f_recv.at[u, m]
                    ).start()

    def whole(src, dst, send, recv):
        return pltpu.make_async_remote_copy(
            src, dst, send, recv, device_id=other, device_id_type=MESH
        )

    def arrange_line(u, dx, dy, m):
        p = line(x - dx, y - dy)[2]
        part = pl.ds(p, 8)
        whole(fsend.at[u, part], frecv.at[u, part], f_send.at[u], f_recv.at[u, m]).wait_recv()
        rr, g = p // 16, (p // 8) % 2
        rows = pl.ds(pl.multiple_of(rr * 32, 32), 32)
        lanes = pl.ds(pl.multiple_of(g * 128, 128), 128)
        for t in range(2):
            swapped = chunk_swap([frecv[u, p + 2 * k + t].astype(F32) for k in range(4)])
            left[u, t, rows, lanes] = jnp.concatenate([v[:8] for v in swapped], axis=0).astype(BF16)
            right[u, t, rows, lanes] = jnp.concatenate([v[8:] for v in swapped], axis=0).astype(BF16)
        whole(
            right.at[u, :, rows, lanes], right_in.at[u, :, rows, lanes], x_send.at[u], x_recv.at[u]
        ).start()
        if u == 1:
            whole(
                left.at[u, 1 - core, rows, lanes], left_in.at[rows, lanes], x_send.at[2], x_recv.at[2]
            ).start()

    def send_sums(u, ts):
        ts = list(ts)

        @pl.loop(0, 16)
        def _(n):
            to_row, base, p = line(x + far_first(n // 4), y + far_first(n % 4))
            rr, g = p // 16, (p // 8) % 2
            lanes = pl.ds(pl.multiple_of(g * 128, 128), 128)
            for t in ts:
                tiles = [
                    sums[t, pl.ds(pl.multiple_of(rr * 32, 32) + 8 * k, 8), lanes] for k in range(4)
                ]
                for k, tile in enumerate(chunk_swap(tiles)):
                    bsend[u, p + 2 * k + t] = tile.astype(BF16)
            for t in ts:
                for d in (4, 2, 6, 0):
                    to_z = (z + d + (z + t) % 2) % 8
                    to = p + to_z

                    def send():
                        pltpu.make_async_remote_copy(
                            bsend.at[u, to], brecv.at[u, chip], b_send.at[u], b_recv.at[u],
                            device_id=(to_row, base + to_z), device_id_type=MESH,
                        ).start()

                    if d:
                        send()
                    else:
                        here = to == chip
                        pl.when(jnp.logical_not(here))(send)

                        @pl.when(here)
                        def _():
                            pltpu.make_async_copy(
                                bsend.at[u, to], brecv.at[u, chip], b_recv.at[u]
                            ).start()

    def receive_sums(u):
        whole(bsend.at[u], brecv.at[u], b_send.at[u], b_recv.at[u]).wait_recv()
        wide[...] = brecv[u].astype(F32).reshape(1024, 128)

    def finish(u, s):
        summed = wide[pl.ds(s, 128, stride=8), :]
        lifted = normalize(summed, gb[4 * u + 2], gb[4 * u + 3]).astype(BF16)
        update = close[s] * dot(ft[u], lifted, ((1,), (0,)))
        return (zt[s].astype(F32) + update).astype(BF16)

    prepare(0)
    for s in range(8):
        z_s = jnp.concatenate([x_ref[8 * k + s] for k in range(4)], axis=0).T
        zt[s] = z_s
        project(0, s, z_s.astype(F32))

    pl.semaphore_wait(barrier, 35)
    for dx in (2, 1, 3):
        to_row, base, _ = line(x + dx, y)
        pl.semaphore_signal(
            entry.at[dx], inc=1, device_id=(to_row, base + z), device_id_type=MESH
        )
    near_first = (0, 1, 3, 2)
    for k, dx in enumerate(near_first):
        if dx:
            pl.semaphore_wait(entry.at[4 - dx], 1)

        @pl.loop(0, 4)
        def _(n):
            send_line(0, dx, far_first(n), 4 * k + n)

    prepare(1)
    for k, dx in enumerate(near_first):

        @pl.loop(0, 4)
        def _(n):
            arrange_line(0, dx, far_first(n), 4 * k + n)

    swap = whole(right.at[0], right_in.at[0], x_send.at[0], x_recv.at[0])

    def outgoing(t, operand):
        sums[t] = dot(left[0, 0], operand[0], ((1,), (1,))) + dot(
            left[0, 1], operand[1], ((1,), (1,))
        )

    outgoing(core, right.at[0])
    send_sums(0, [core])
    swap.wait_recv()
    outgoing(1 - core, right_in.at[0])
    send_sums(0, [1 - core])
    receive_sums(0)

    for s in range(8):
        z_s = finish(0, s)
        zt[s] = z_s
        project(1, s, z_s.astype(F32))

    @pl.loop(0, 16)
    def _(n):
        send_line(1, far_first(n // 4), far_first(n % 4), n)

    @pl.loop(0, 16)
    def _(n):
        arrange_line(1, far_first(n // 4), far_first(n % 4), n)

    swap_left = whole(left.at[1, 1 - core], left_in, x_send.at[2], x_recv.at[2])
    swap_right = whole(right.at[1], right_in.at[1], x_send.at[1], x_recv.at[1])
    for t in range(2):
        sums[t] = dot(left[1, core], right[1, t], ((0,), (0,)))
    swap_left.wait_recv()
    swap_right.wait_recv()
    for t in range(2):
        sums[t] = sums[t] + dot(left_in[...], right_in[1, t], ((0,), (0,)))
    send_sums(1, [0, 1])
    receive_sums(1)

    for s in range(8):
        z_s = finish(1, s).T
        for k in range(4):
            out_ref[8 * k + s] = z_s[32 * k : 32 * k + 32]

    swap.wait_send()
    swap_left.wait_send()
    swap_right.wait_send()
    most = pl.ds(0, 127)
    for u in range(2):
        whole(fsend.at[u, most], frecv.at[u, most], f_send.at[u], f_recv.at[u, 0]).wait_send()
        whole(bsend.at[u, most], brecv.at[u, most], b_send.at[u], b_recv.at[u]).wait_send()


def shards(*arrays):
    vmem = pl.BlockSpec(memory_space=pltpu.VMEM)
    hbm = pl.BlockSpec(memory_space=pltpu.HBM)
    return pl.pallas_call(
        kernel,
        out_shape=jax.ShapeDtypeStruct(arrays[0].shape, BF16),
        in_specs=[hbm] * 10,
        out_specs=vmem,
        scratch_shapes=[
            (pltpu.SMEM if array.ndim == 1 else pltpu.VMEM)(array.shape, array.dtype)
            for array in arrays
        ]
        + [
            pltpu.VMEM((2, 640, 128), BF16),
            pltpu.VMEM((2, 128, 128), BF16),
            pltpu.VMEM((8, 128, 128), F32),
            pltpu.VMEM((8, 128, 128), BF16),
            pltpu.VMEM((8, 128, 128), F32),
            pltpu.VMEM((2048, 128), F32),
            pltpu.VMEM((2, 128, 16, 128), BF16),
            pltpu.VMEM((2, 128, 16, 128), BF16),
            pltpu.VMEM((2, 2, 256, 256), BF16),
            pltpu.VMEM((2, 2, 256, 256), BF16),
            pltpu.VMEM((256, 256), BF16),
            pltpu.VMEM((2, 2, 256, 256), BF16),
            pltpu.VMEM((2, 256, 256), F32),
            pltpu.VMEM((2, 128, 8, 128), BF16),
            pltpu.VMEM((2, 128, 8, 128), BF16),
            pltpu.VMEM((1024, 128), F32),
            pltpu.SemaphoreType.DMA((10,)),
            pltpu.SemaphoreType.REGULAR((4,)),
            pltpu.SemaphoreType.DMA((2,)),
            pltpu.SemaphoreType.DMA((2, 16)),
            pltpu.SemaphoreType.DMA((2,)),
            pltpu.SemaphoreType.DMA((2,)),
            pltpu.SemaphoreType.DMA((3,)),
            pltpu.SemaphoreType.DMA((3,)),
        ],
        compiler_params=pltpu.CompilerParams(
            collective_id=0, has_side_effects=True, vmem_limit_bytes=32 << 20
        ),
    )(*arrays)


def solution(mesh):
    return jax.shard_map(
        shards,
        mesh=mesh,
        in_specs=(P("row", "col", None), P(), P(), P(), P(), P(), P(), P(), P(), P()),
        out_specs=P("row", "col", None),
        check_vma=False,
    )
```

```python
import jax
import jax.numpy as jnp
from jax import lax
from jax.experimental import pallas as pl
from jax.experimental.pallas import tpu as pltpu
from jax.sharding import PartitionSpec as P

MESH = pl.DeviceIdType.MESH
F32 = jnp.float32
BF16 = jnp.bfloat16


def far_first(n):
    return n + 2 - (n // 2) * (2 * n - 1)


def dot(a, b, dims):
    return lax.dot_general(a, b, (dims, ((), ())), preferred_element_type=F32)


def sigmoid(v):
    return 0.5 * jnp.tanh(0.5 * v) + 0.5


def normalize(v, gain, bias):
    average = jnp.mean(v, axis=0, keepdims=True)
    centred = v - average
    variance = jnp.mean(centred * centred, axis=0, keepdims=True)
    return centred * lax.rsqrt(variance + 1e-05) * gain + bias


def chunk_swap(v):
    lane = lax.broadcasted_iota(jnp.int32, v[0].shape, 1)
    odd = (lane // 32) % 2 == 1
    high = lane >= 64

    def pair(a, b, shift, mask):
        return jnp.where(mask, pltpu.roll(b, shift, 1), a), jnp.where(
            mask, b, pltpu.roll(a, 128 - shift, 1)
        )

    a, b = pair(v[0], v[1], 32, odd)
    c, d = pair(v[2], v[3], 32, odd)
    a, c = pair(a, c, 64, high)
    b, d = pair(b, d, 64, high)
    return a, b, c, d


def kernel(
    x_hbm, mask_hbm, ng_hbm, nb_hbm, pw_hbm, gw_hbm, og_hbm, ob_hbm, fw_hbm, ow_hbm,
    out_ref,
    x_ref, mask_ref, ng_ref, nb_ref, pw_ref, gw_ref, og_ref, ob_ref, fw_ref, ow_ref,
    wt, ft, gb, zt, close, half, fsend, frecv, left, right, left_in, right_in, sums, bsend, brecv, wide,
    in_sem, entry, f_send, f_recv, b_send, b_recv, x_send, x_recv,
):
    row, col = lax.axis_index("row"), lax.axis_index("col")
    core = row % 2
    x, y, z = (row // 8) * 2 + col // 8, (row // 2) % 4, col % 8
    other = (row + 1 - 2 * core, col)

    hbm = (x_hbm, mask_hbm, ng_hbm, nb_hbm, pw_hbm, gw_hbm, og_hbm, ob_hbm, fw_hbm, ow_hbm)
    held = (x_ref, mask_ref, ng_ref, nb_ref, pw_ref, gw_ref, og_ref, ob_ref, fw_ref, ow_ref)
    inputs = [
        pltpu.make_async_copy(a, b, in_sem.at[k]) for k, (a, b) in enumerate(zip(hbm, held))
    ]
    for copy in inputs:
        copy.start()

    def line(x, y):
        x, y = (x + 4) % 4, (y + 4) % 4
        rr, base = (x // 2) * 4 + y, (x % 2) * 8
        return rr * 2 + core, base, rr * 16 + base

    chip = line(x, y)[2] + z
    ring = [(z + d) % 8 for d in range(8)]
    outward = (4, 3, 5, 2, 6, 1, 7, 0)

    barrier = pltpu.get_barrier_semaphore()
    for dx in (2, 1, 3):
        to_row, base, _ = line(x + dx, y)
        pl.semaphore_signal(barrier, inc=1, device_id=(to_row, base + z), device_id_type=MESH)
    for dy in (2, 1, 3, 0):
        to_row, base, _ = line(x, y + dy)
        for dz in outward[: 8 if dy else 7]:
            pl.semaphore_signal(
                barrier, inc=1, device_id=(to_row, base + ring[dz]), device_id_type=MESH
            )
    pl.semaphore_signal(barrier, inc=1, device_id=other, device_id_type=MESH)

    for copy in inputs:
        copy.wait()

    lane = lax.broadcasted_iota(jnp.int32, (8, 128), 1)
    first = lax.broadcasted_iota(jnp.int32, (8, 128), 0) + 8 * (lane // 32)
    row_mask = jnp.zeros((8, 128), jnp.int32)
    col_mask = jnp.zeros((8, 128), jnp.int32)
    for a in range(32):
        row_mask = jnp.where(first == a, mask_ref[row * 32 + a], row_mask)
        col_mask = jnp.where(lane % 32 == a, mask_ref[col * 32 + a], col_mask)
    token_mask = row_mask.astype(F32) * col_mask.astype(F32)

    def prepare(u):
        for k in range(2):
            wt[u, pl.ds(128 * k, 128)] = pw_ref[u, :, pl.ds(128 * k, 128)].T
            wt[u, pl.ds(256 + 128 * k, 128)] = gw_ref[u, :, pl.ds(128 * k, 128)].T
        wt[u, pl.ds(512, 128)] = ow_ref[u].T
        ft[u] = fw_ref[u].T
        for k, ref in enumerate((ng_ref, nb_ref, og_ref, ob_ref)):
            gb[4 * u + k] = jnp.broadcast_to(ref[pl.ds(u, 1), :], (128, 128)).T

    def project(u, s, z_s):
        normed = normalize(z_s, gb[4 * u], gb[4 * u + 1]).astype(BF16)
        product = dot(wt[u], normed, ((1,), (0,)))
        close[s] = sigmoid(product[512:])
        half[pl.ds(s, 256, stride=8), :] = (
            sigmoid(product[256:512]) * product[:256] * token_mask[s : s + 1]
        )

    def send_line(u, dx, dy, m):
        to_row, base, p = line(x + dx, y + dy)
        rows = pl.multiple_of(p * 8, 64)
        fsend[u, pl.ds(p, 8)] = jnp.concatenate(
            [
                half[pl.ds(rows, 64), :].reshape(8, 8, 128),
                half[pl.ds(rows + 1024, 64), :].reshape(8, 8, 128),
            ],
            axis=1,
        ).astype(BF16)
        for dz in outward:
            to = p + ring[dz]

            def send():
                pltpu.make_async_remote_copy(
                    fsend.at[u, to], frecv.at[u, chip], f_send.at[u], f_recv.at[u, m],
                    device_id=(to_row, base + ring[dz]), device_id_type=MESH,
                ).start()

            if dz:
                send()
            else:
                here = to == chip
                pl.when(jnp.logical_not(here))(send)

                @pl.when(here)
                def _():
                    pltpu.make_async_copy(
                        fsend.at[u, to], frecv.at[u, chip], f_recv.at[u, m]
                    ).start()

    def whole(src, dst, send, recv):
        return pltpu.make_async_remote_copy(
            src, dst, send, recv, device_id=other, device_id_type=MESH
        )

    def arrange_line(u, dx, dy, m):
        p = line(x - dx, y - dy)[2]
        part = pl.ds(p, 8)
        whole(fsend.at[u, part], frecv.at[u, part], f_send.at[u], f_recv.at[u, m]).wait_recv()
        rr, g = p // 16, (p // 8) % 2
        rows = pl.ds(pl.multiple_of(rr * 32, 32), 32)
        lanes = pl.ds(pl.multiple_of(g * 128, 128), 128)
        for t in range(2):
            swapped = chunk_swap([frecv[u, p + 2 * k + t].astype(F32) for k in range(4)])
            left[u, t, rows, lanes] = jnp.concatenate([v[:8] for v in swapped], axis=0).astype(BF16)
            right[u, t, rows, lanes] = jnp.concatenate([v[8:] for v in swapped], axis=0).astype(BF16)
        whole(
            right.at[u, :, rows, lanes], right_in.at[u, :, rows, lanes], x_send.at[u], x_recv.at[u]
        ).start()
        if u == 1:
            whole(
                left.at[u, 1 - core, rows, lanes], left_in.at[rows, lanes], x_send.at[2], x_recv.at[2]
            ).start()

    def send_sums(u, ts):
        ts = list(ts)

        @pl.loop(0, 16)
        def _(n):
            to_row, base, p = line(x + far_first(n // 4), y + far_first(n % 4))
            rr, g = p // 16, (p // 8) % 2
            lanes = pl.ds(pl.multiple_of(g * 128, 128), 128)
            for t in ts:
                tiles = [
                    sums[t, pl.ds(pl.multiple_of(rr * 32, 32) + 8 * k, 8), lanes] for k in range(4)
                ]
                for k, tile in enumerate(chunk_swap(tiles)):
                    bsend[u, p + 2 * k + t] = tile.astype(BF16)
            for t in ts:
                for d in (4, 2, 6, 0):
                    to_z = (z + d + (z + t) % 2) % 8
                    to = p + to_z

                    def send():
                        pltpu.make_async_remote_copy(
                            bsend.at[u, to], brecv.at[u, chip], b_send.at[u], b_recv.at[u],
                            device_id=(to_row, base + to_z), device_id_type=MESH,
                        ).start()

                    if d:
                        send()
                    else:
                        here = to == chip
                        pl.when(jnp.logical_not(here))(send)

                        @pl.when(here)
                        def _():
                            pltpu.make_async_copy(
                                bsend.at[u, to], brecv.at[u, chip], b_recv.at[u]
                            ).start()

    def receive_sums(u):
        whole(bsend.at[u], brecv.at[u], b_send.at[u], b_recv.at[u]).wait_recv()
        wide[...] = brecv[u].astype(F32).reshape(1024, 128)

    def finish(u, s):
        summed = wide[pl.ds(s, 128, stride=8), :]
        lifted = normalize(summed, gb[4 * u + 2], gb[4 * u + 3]).astype(BF16)
        update = close[s] * dot(ft[u], lifted, ((1,), (0,)))
        return (zt[s].astype(F32) + update).astype(BF16)

    prepare(0)
    for s in range(8):
        z_s = jnp.concatenate([x_ref[8 * k + s] for k in range(4)], axis=0).T
        zt[s] = z_s
        project(0, s, z_s.astype(F32))

    pl.semaphore_wait(barrier, 35)
    for dx in (2, 1, 3):
        to_row, base, _ = line(x + dx, y)
        pl.semaphore_signal(
            entry.at[dx], inc=1, device_id=(to_row, base + z), device_id_type=MESH
        )

    def outer(n):
        return far_first(n % 3), far_first((n // 3 + n % 3) % 4), 4 + n

    @pl.loop(0, 4)
    def _(n):
        send_line(0, 0, far_first(n), n)

    for dx in (2, 1, 3):
        pl.semaphore_wait(entry.at[dx], 1)

    @pl.loop(0, 12)
    def _(n):
        send_line(0, *outer(n))

    prepare(1)

    @pl.loop(0, 4)
    def _(n):
        arrange_line(0, 0, far_first(n), n)

    @pl.loop(0, 12)
    def _(n):
        arrange_line(0, *outer(n))

    swap = whole(right.at[0], right_in.at[0], x_send.at[0], x_recv.at[0])

    def outgoing(t, operand):
        sums[t] = dot(left[0, 0], operand[0], ((1,), (1,))) + dot(
            left[0, 1], operand[1], ((1,), (1,))
        )

    outgoing(core, right.at[0])
    send_sums(0, [core])
    swap.wait_recv()
    outgoing(1 - core, right_in.at[0])
    send_sums(0, [1 - core])
    receive_sums(0)

    for s in range(8):
        z_s = finish(0, s)
        zt[s] = z_s
        project(1, s, z_s.astype(F32))

    def mixed(n):
        return far_first(n % 4), far_first((n // 4 + n) % 4), n

    @pl.loop(0, 16)
    def _(n):
        send_line(1, *mixed(n))

    @pl.loop(0, 16)
    def _(n):
        arrange_line(1, *mixed(n))

    swap_left = whole(left.at[1, 1 - core], left_in, x_send.at[2], x_recv.at[2])
    swap_right = whole(right.at[1], right_in.at[1], x_send.at[1], x_recv.at[1])
    for t in range(2):
        sums[t] = dot(left[1, core], right[1, t], ((0,), (0,)))
    swap_left.wait_recv()
    swap_right.wait_recv()
    for t in range(2):
        sums[t] = sums[t] + dot(left_in[...], right_in[1, t], ((0,), (0,)))
    send_sums(1, [0, 1])
    receive_sums(1)

    for s in range(8):
        z_s = finish(1, s).T
        for k in range(4):
            out_ref[8 * k + s] = z_s[32 * k : 32 * k + 32]

    swap.wait_send()
    swap_left.wait_send()
    swap_right.wait_send()
    most = pl.ds(0, 127)
    for u in range(2):
        whole(fsend.at[u, most], frecv.at[u, most], f_send.at[u], f_recv.at[u, 0]).wait_send()
        whole(bsend.at[u, most], brecv.at[u, most], b_send.at[u], b_recv.at[u]).wait_send()


def shards(*arrays):
    vmem = pl.BlockSpec(memory_space=pltpu.VMEM)
    hbm = pl.BlockSpec(memory_space=pltpu.HBM)
    return pl.pallas_call(
        kernel,
        out_shape=jax.ShapeDtypeStruct(arrays[0].shape, BF16),
        in_specs=[hbm] * 10,
        out_specs=vmem,
        scratch_shapes=[
            (pltpu.SMEM if array.ndim == 1 else pltpu.VMEM)(array.shape, array.dtype)
            for array in arrays
        ]
        + [
            pltpu.VMEM((2, 640, 128), BF16),
            pltpu.VMEM((2, 128, 128), BF16),
            pltpu.VMEM((8, 128, 128), F32),
            pltpu.VMEM((8, 128, 128), BF16),
            pltpu.VMEM((8, 128, 128), F32),
            pltpu.VMEM((2048, 128), F32),
            pltpu.VMEM((2, 128, 16, 128), BF16),
            pltpu.VMEM((2, 128, 16, 128), BF16),
            pltpu.VMEM((2, 2, 256, 256), BF16),
            pltpu.VMEM((2, 2, 256, 256), BF16),
            pltpu.VMEM((256, 256), BF16),
            pltpu.VMEM((2, 2, 256, 256), BF16),
            pltpu.VMEM((2, 256, 256), F32),
            pltpu.VMEM((2, 128, 8, 128), BF16),
            pltpu.VMEM((2, 128, 8, 128), BF16),
            pltpu.VMEM((1024, 128), F32),
            pltpu.SemaphoreType.DMA((10,)),
            pltpu.SemaphoreType.REGULAR((4,)),
            pltpu.SemaphoreType.DMA((2,)),
            pltpu.SemaphoreType.DMA((2, 16)),
            pltpu.SemaphoreType.DMA((2,)),
            pltpu.SemaphoreType.DMA((2,)),
            pltpu.SemaphoreType.DMA((3,)),
            pltpu.SemaphoreType.DMA((3,)),
        ],
        compiler_params=pltpu.CompilerParams(
            collective_id=0, has_side_effects=True, vmem_limit_bytes=32 << 20
        ),
    )(*(pltpu.with_memory_space_constraint(array, pltpu.HBM) for array in arrays))


def solution(mesh):
    return jax.shard_map(
        shards,
        mesh=mesh,
        in_specs=(P("row", "col", None), P(), P(), P(), P(), P(), P(), P(), P(), P()),
        out_specs=P("row", "col", None),
        check_vma=False,
    )
```

```python
import jax
import jax.numpy as jnp
from jax import lax
from jax.experimental import pallas as pl
from jax.experimental.pallas import tpu as pltpu
from jax.sharding import PartitionSpec as P

MESH = pl.DeviceIdType.MESH
F32 = jnp.float32
BF16 = jnp.bfloat16


def far_first(n):
    return n + 2 - (n // 2) * (2 * n - 1)


def dot(a, b, dims):
    return lax.dot_general(a, b, (dims, ((), ())), preferred_element_type=F32)


def sigmoid(v):
    return 0.5 * jnp.tanh(0.5 * v) + 0.5


def normalize(v, gain, bias):
    average = jnp.mean(v, axis=0, keepdims=True)
    centred = v - average
    variance = jnp.mean(centred * centred, axis=0, keepdims=True)
    return centred * lax.rsqrt(variance + 1e-05) * gain + bias


def chunk_swap(v):
    lane = lax.broadcasted_iota(jnp.int32, v[0].shape, 1)
    odd = (lane // 32) % 2 == 1
    high = lane >= 64

    def pair(a, b, shift, mask):
        return jnp.where(mask, pltpu.roll(b, shift, 1), a), jnp.where(
            mask, b, pltpu.roll(a, 128 - shift, 1)
        )

    a, b = pair(v[0], v[1], 32, odd)
    c, d = pair(v[2], v[3], 32, odd)
    a, c = pair(a, c, 64, high)
    b, d = pair(b, d, 64, high)
    return a, b, c, d


def kernel(
    x_hbm, mask_hbm, ng_hbm, nb_hbm, pw_hbm, gw_hbm, og_hbm, ob_hbm, fw_hbm, ow_hbm,
    out_ref,
    x_ref, mask_ref, ng_ref, nb_ref, pw_ref, gw_ref, og_ref, ob_ref, fw_ref, ow_ref,
    wt, ft, gb, zt, close, half, fsend, frecv, lrecv, lrecv_1, left, right, right_in, turned, sums, bsend, brecv, wide,
    in_sem, entry, f_send, f_recv, l_send, l_recv, l_recv_1, b_send, b_recv, x_send, x_recv,
):
    row, col = lax.axis_index("row"), lax.axis_index("col")
    core = row % 2
    x, y, z = (row // 8) * 2 + col // 8, (row // 2) % 4, col % 8
    other = (row + 1 - 2 * core, col)

    hbm = (x_hbm, mask_hbm, ng_hbm, nb_hbm, pw_hbm, gw_hbm, og_hbm, ob_hbm, fw_hbm, ow_hbm)
    held = (x_ref, mask_ref, ng_ref, nb_ref, pw_ref, gw_ref, og_ref, ob_ref, fw_ref, ow_ref)
    inputs = [
        pltpu.make_async_copy(a, b, in_sem.at[k]) for k, (a, b) in enumerate(zip(hbm, held))
    ]
    for copy in inputs:
        copy.start()

    def line(x, y):
        x, y = (x + 4) % 4, (y + 4) % 4
        rr, base = (x // 2) * 4 + y, (x % 2) * 8
        return rr * 2 + core, base, rr * 16 + base

    chip = line(x, y)[2] + z
    ring = [(z + d) % 8 for d in range(8)]
    outward = (4, 3, 5, 2, 6, 1, 7, 0)

    barrier = pltpu.get_barrier_semaphore()
    for dx in (2, 1, 3):
        to_row, base, _ = line(x + dx, y)
        pl.semaphore_signal(barrier, inc=1, device_id=(to_row, base + z), device_id_type=MESH)
    for dy in (2, 1, 3, 0):
        to_row, base, _ = line(x, y + dy)
        for dz in outward[: 8 if dy else 7]:
            pl.semaphore_signal(
                barrier, inc=1, device_id=(to_row, base + ring[dz]), device_id_type=MESH
            )
    pl.semaphore_signal(barrier, inc=1, device_id=other, device_id_type=MESH)

    for copy in inputs:
        copy.wait()

    lane = lax.broadcasted_iota(jnp.int32, (8, 128), 1)
    first = lax.broadcasted_iota(jnp.int32, (8, 128), 0) + 8 * (lane // 32)
    row_mask = jnp.zeros((8, 128), jnp.int32)
    col_mask = jnp.zeros((8, 128), jnp.int32)
    for a in range(32):
        row_mask = jnp.where(first == a, mask_ref[row * 32 + a], row_mask)
        col_mask = jnp.where(lane % 32 == a, mask_ref[col * 32 + a], col_mask)
    token_mask = row_mask.astype(F32) * col_mask.astype(F32)

    def prepare(u):
        for k in range(2):
            wt[u, pl.ds(128 * k, 128)] = pw_ref[u, :, pl.ds(128 * k, 128)].T
            wt[u, pl.ds(256 + 128 * k, 128)] = gw_ref[u, :, pl.ds(128 * k, 128)].T
        wt[u, pl.ds(512, 128)] = ow_ref[u].T
        ft[u] = fw_ref[u].T
        for k, ref in enumerate((ng_ref, nb_ref, og_ref, ob_ref)):
            gb[4 * u + k] = jnp.broadcast_to(ref[pl.ds(u, 1), :], (128, 128)).T

    def project(u, s, z_s):
        normed = normalize(z_s, gb[4 * u], gb[4 * u + 1]).astype(BF16)
        product = dot(wt[u], normed, ((1,), (0,)))
        close[s] = sigmoid(product[512:])
        half[pl.ds(s, 256, stride=8), :] = (
            sigmoid(product[256:512]) * product[:256] * token_mask[s : s + 1]
        )

    def pack(u, side, p):
        rows = pl.multiple_of(p * 8, 64)
        fsend[u, side, pl.ds(p, 8)] = (
            half[pl.ds(rows + 1024 * side, 64), :].reshape(8, 8, 128).astype(BF16)
        )

    def send_tile(src, dst, send_sem, recv_sem, device, here):
        def send():
            pltpu.make_async_remote_copy(
                src, dst, send_sem, recv_sem, device_id=device, device_id_type=MESH
            ).start()

        if here is False:
            send()
        else:
            pl.when(jnp.logical_not(here))(send)

            @pl.when(here)
            def _():
                pltpu.make_async_copy(src, dst, recv_sem).start()

    def send_right(u, dx, dy, m):
        to_row, base, p = line(x + dx, y + dy)
        pack(u, 1, p)
        for dz in outward:
            to = p + ring[dz]
            send_tile(
                fsend.at[u, 1, to], frecv.at[u, chip], f_send.at[u], f_recv.at[u, m],
                (to_row, base + ring[dz]), False if dz else to == chip,
            )

    def whole(src, dst, send, recv):
        return pltpu.make_async_remote_copy(
            src, dst, send, recv, device_id=other, device_id_type=MESH
        )

    def arrange(tiles):
        return jnp.concatenate(chunk_swap([v.astype(F32) for v in tiles]), axis=0).astype(BF16)

    def arrange_right(u, dx, dy, m):
        p = line(x - dx, y - dy)[2]
        part = frecv.at[u, pl.ds(p, 8)]
        whole(part, part, f_send.at[u], f_recv.at[u, m]).wait_recv()
        rr, g = p // 16, (p // 8) % 2
        rows = pl.ds(pl.multiple_of(rr * 32, 32), 32)
        lanes = pl.ds(pl.multiple_of(g * 128, 128), 128)
        for t in range(2):
            right[u, t, rows, lanes] = arrange([frecv[u, p + 2 * k + t] for k in range(4)])
        whole(
            right.at[u, :, rows, lanes], right_in.at[u, :, rows, lanes], x_send.at[u], x_recv.at[u]
        ).start()

    def send_rows(u, rr, first_row, ts):
        for t in ts:
            for g in range(2):
                tiles = [
                    sums[t, pl.ds(first_row + 8 * k, 8), pl.ds(128 * g, 128)] for k in range(4)
                ]
                for k, tile in enumerate(chunk_swap(tiles)):
                    bsend[u, rr * 16 + 8 * g + 2 * k + t] = tile.astype(BF16)
        for d in (1, 0):
            base = ((col // 8 + d) % 2) * 8
            for dz in outward:
                to = rr * 16 + base + ring[dz]
                send_tile(
                    bsend.at[u, to], brecv.at[u, chip], b_send.at[u], b_recv.at[u],
                    (rr * 2 + core, base + ring[dz]), False if d or dz else to == chip,
                )

    def receive_sums(u):
        whole(bsend.at[u], brecv.at[u], b_send.at[u], b_recv.at[u]).wait_recv()
        wide[...] = brecv[u].astype(F32).reshape(1024, 128)

    def finish(u, s):
        summed = wide[pl.ds(s, 128, stride=8), :]
        lifted = normalize(summed, gb[4 * u + 2], gb[4 * u + 3]).astype(BF16)
        update = close[s] * dot(ft[u], lifted, ((1,), (0,)))
        return (zt[s].astype(F32) + update).astype(BF16)

    prepare(0)
    for s in range(8):
        z_s = jnp.concatenate([x_ref[8 * k + s] for k in range(4)], axis=0).T
        zt[s] = z_s
        project(0, s, z_s.astype(F32))

    pl.semaphore_wait(barrier, 35)
    for dx in (2, 1, 3):
        to_row, base, _ = line(x + dx, y)
        pl.semaphore_signal(
            entry.at[dx], inc=1, device_id=(to_row, base + z), device_id_type=MESH
        )

    def outer(n):
        return far_first(n % 3), far_first((n // 3 + n % 3) % 4), 4 + n

    @pl.loop(0, 4)
    def _(n):
        send_right(0, 0, far_first(n), n)

    for dx in (2, 1, 3):
        pl.semaphore_wait(entry.at[dx], 1)

    @pl.loop(0, 12)
    def _(n):
        send_right(0, *outer(n))

    def part_of(n):
        return (x // 2 + 1 - n // 4) % 2, far_first(n % 4)

    @pl.loop(0, 8)
    def _(n):
        x_hi, dy = part_of(n)
        for d in (1, 0):
            to_row, base, p = line(2 * x_hi + (x + d) % 2, y + dy)
            pack(0, 0, p)
            for dz in outward:
                to = p + ring[dz]
                send_tile(
                    fsend.at[0, 0, to], lrecv.at[chip], l_send.at[0], l_recv.at[n],
                    (to_row, base + ring[dz]), False if d or dz else to == chip,
                )

    prepare(1)

    @pl.loop(0, 4)
    def _(n):
        arrange_right(0, 0, far_first(n), n)

    @pl.loop(0, 12)
    def _(n):
        arrange_right(0, *outer(n))

    swap = whole(right.at[0], right_in.at[0], x_send.at[0], x_recv.at[0])
    for t in range(2):
        turned[core, t] = right[0, t].T
    swap.wait_recv()
    for t in range(2):
        turned[1 - core, t] = right_in[0, t].T

    @pl.loop(0, 8)
    def _(n):
        x_hi, dy = part_of(n)
        rr = x_hi * 4 + (y + 4 - dy) % 4
        part = lrecv.at[pl.ds(rr * 16, 16)]
        whole(part, part, l_send.at[0], l_recv.at[n]).wait_recv()
        rows = [
            jnp.concatenate(
                [arrange([lrecv[rr * 16 + 8 * g + 2 * k + t] for k in range(4)]) for g in range(2)],
                axis=1,
            )
            for t in range(2)
        ]
        for t in range(2):
            sums[t, pl.ds(0, 32)] = dot(rows[0], turned[t, 0], ((1,), (0,))) + dot(
                rows[1], turned[t, 1], ((1,), (0,))
            )
        send_rows(0, rr, 0, range(2))

    receive_sums(0)

    for s in range(8):
        z_s = finish(0, s)
        zt[s] = z_s
        project(1, s, z_s.astype(F32))

    def mixed(n):
        return far_first(n % 4), far_first((n // 4 + n) % 4), n

    @pl.loop(0, 16)
    def _(n):
        send_right(1, *mixed(n))

    summing = z % 2

    @pl.loop(0, 2)
    def _(n):
        x_hi = (x + 1 + n) % 2

        @pl.loop(0, 8)
        def _(k):
            x_lo = (x + 1 + k // 4) % 2
            to_row, base, p = line(2 * x_hi + x_lo, y + far_first(k % 4))
            to_row = to_row - core + summing
            pack(1, 0, p)
            for dz in outward:
                to = p + ring[dz]
                here = jnp.logical_and(to == chip, summing == core)
                send_tile(
                    fsend.at[1, 0, to], lrecv_1.at[core, chip], l_send.at[1], l_recv_1.at[n],
                    (to_row, base + ring[dz]), False if dz else here,
                )

    @pl.loop(0, 16)
    def _(n):
        arrange_right(1, *mixed(n))

    swap_1 = whole(right.at[1], right_in.at[1], x_send.at[1], x_recv.at[1])
    swap_1.wait_recv()

    @pl.loop(0, 2)
    def _(n):
        g = (x // 2 + 1 - n) % 2
        part = lrecv_1.at[0, pl.ds(0, 64)]
        whole(part, part, l_send.at[1], l_recv_1.at[n]).wait_recv()

        @pl.loop(0, 8)
        def _(rr):
            rows = pl.ds(pl.multiple_of(rr * 32, 32), 32)
            for c in range(2):
                left[c, rows, :] = arrange(
                    [lrecv_1[c, rr * 16 + 8 * g + 2 * k + core] for k in range(4)]
                )

        for t in range(2):
            sums[t] = dot(left[core], right[1, t], ((0,), (0,))) + dot(
                left[1 - core], right_in[1, t], ((0,), (0,))
            )

        @pl.loop(0, 4)
        def _(k):
            to_y = (y + far_first(k)) % 4
            send_rows(1, g * 4 + to_y, pl.multiple_of(to_y * 32, 32), range(2))

    receive_sums(1)

    for s in range(8):
        z_s = finish(1, s).T
        for k in range(4):
            out_ref[8 * k + s] = z_s[32 * k : 32 * k + 32]

    swap.wait_send()
    swap_1.wait_send()
    most = pl.ds(0, 127)
    for u in range(2):
        for side, send in ((1, f_send), (0, l_send)):
            sent = fsend.at[u, side, most]
            whole(sent, sent, send.at[u], f_recv.at[u, 0]).wait_send()
        whole(bsend.at[u, most], brecv.at[u, most], b_send.at[u], b_recv.at[u]).wait_send()

    @pl.when(summing != core)
    def _():
        sent = fsend.at[1, 0, 0]
        whole(sent, sent, l_send.at[1], f_recv.at[1, 0]).wait_send()


def shards(*arrays):
    vmem = pl.BlockSpec(memory_space=pltpu.VMEM)
    hbm = pl.BlockSpec(memory_space=pltpu.HBM)
    return pl.pallas_call(
        kernel,
        out_shape=jax.ShapeDtypeStruct(arrays[0].shape, BF16),
        in_specs=[hbm] * 10,
        out_specs=vmem,
        scratch_shapes=[
            (pltpu.SMEM if array.ndim == 1 else pltpu.VMEM)(array.shape, array.dtype)
            for array in arrays
        ]
        + [
            pltpu.VMEM((2, 640, 128), BF16),
            pltpu.VMEM((2, 128, 128), BF16),
            pltpu.VMEM((8, 128, 128), F32),
            pltpu.VMEM((8, 128, 128), BF16),
            pltpu.VMEM((8, 128, 128), F32),
            pltpu.VMEM((2048, 128), F32),
            pltpu.VMEM((2, 2, 128, 8, 128), BF16),
            pltpu.VMEM((2, 128, 8, 128), BF16),
            pltpu.VMEM((128, 8, 128), BF16),
            pltpu.VMEM((2, 128, 8, 128), BF16),
            pltpu.VMEM((2, 256, 128), BF16),
            pltpu.VMEM((2, 2, 256, 256), BF16),
            pltpu.VMEM((2, 2, 256, 256), BF16),
            pltpu.VMEM((2, 2, 256, 256), BF16),
            pltpu.VMEM((2, 128, 256), F32),
            pltpu.VMEM((2, 128, 8, 128), BF16),
            pltpu.VMEM((2, 128, 8, 128), BF16),
            pltpu.VMEM((1024, 128), F32),
            pltpu.SemaphoreType.DMA((10,)),
            pltpu.SemaphoreType.REGULAR((4,)),
            pltpu.SemaphoreType.DMA((2,)),
            pltpu.SemaphoreType.DMA((2, 16)),
            pltpu.SemaphoreType.DMA((2,)),
            pltpu.SemaphoreType.DMA((8,)),
            pltpu.SemaphoreType.DMA((2,)),
            pltpu.SemaphoreType.DMA((2,)),
            pltpu.SemaphoreType.DMA((2,)),
            pltpu.SemaphoreType.DMA((2,)),
            pltpu.SemaphoreType.DMA((2,)),
        ],
        compiler_params=pltpu.CompilerParams(
            collective_id=0, has_side_effects=True, vmem_limit_bytes=32 << 20
        ),
    )(*(pltpu.with_memory_space_constraint(array, pltpu.HBM) for array in arrays))


def solution(mesh):
    return jax.shard_map(
        shards,
        mesh=mesh,
        in_specs=(P("row", "col", None), P(), P(), P(), P(), P(), P(), P(), P(), P()),
        out_specs=P("row", "col", None),
        check_vma=False,
    )
```

```python
import jax
import jax.numpy as jnp
from jax import lax
from jax.experimental import pallas as pl
from jax.experimental.pallas import tpu as pltpu
from jax.sharding import PartitionSpec as P

MESH = pl.DeviceIdType.MESH
F32 = jnp.float32
BF16 = jnp.bfloat16


def far_first(n):
    return n + 2 - (n // 2) * (2 * n - 1)


def dot(a, b, dims):
    return lax.dot_general(a, b, (dims, ((), ())), preferred_element_type=F32)


def sigmoid(v):
    return 0.5 * jnp.tanh(0.5 * v) + 0.5


def normalize(v, gain, bias):
    average = jnp.mean(v, axis=0, keepdims=True)
    centred = v - average
    variance = jnp.mean(centred * centred, axis=0, keepdims=True)
    return centred * lax.rsqrt(variance + 1e-05) * gain + bias


def chunk_swap(v):
    lane = lax.broadcasted_iota(jnp.int32, v[0].shape, 1)
    odd = (lane // 32) % 2 == 1
    high = lane >= 64

    def pair(a, b, shift, mask):
        return jnp.where(mask, pltpu.roll(b, shift, 1), a), jnp.where(
            mask, b, pltpu.roll(a, 128 - shift, 1)
        )

    a, b = pair(v[0], v[1], 32, odd)
    c, d = pair(v[2], v[3], 32, odd)
    a, c = pair(a, c, 64, high)
    b, d = pair(b, d, 64, high)
    return a, b, c, d


def kernel(
    x_hbm, mask_hbm, ng_hbm, nb_hbm, pw_hbm, gw_hbm, og_hbm, ob_hbm, fw_hbm, ow_hbm,
    out_ref,
    x_ref, mask_ref, ng_ref, nb_ref, pw_ref, gw_ref, og_ref, ob_ref, fw_ref, ow_ref,
    wt, ft, gb, zt, close, half, fsend, frecv, lrecv, lrecv_1, left, right, right_in, turned, sums, bsend, brecv, wide,
    in_sem, entry, f_send, f_recv, l_send, l_recv, l_recv_1, b_send, b_recv, x_send, x_recv,
):
    row, col = lax.axis_index("row"), lax.axis_index("col")
    core = row % 2
    x, y, z = (row // 8) * 2 + col // 8, (row // 2) % 4, col % 8
    other = (row + 1 - 2 * core, col)

    hbm = (x_hbm, mask_hbm, ng_hbm, nb_hbm, pw_hbm, gw_hbm, og_hbm, ob_hbm, fw_hbm, ow_hbm)
    held = (x_ref, mask_ref, ng_ref, nb_ref, pw_ref, gw_ref, og_ref, ob_ref, fw_ref, ow_ref)
    inputs = [
        pltpu.make_async_copy(a, b, in_sem.at[k]) for k, (a, b) in enumerate(zip(hbm, held))
    ]
    for copy in inputs:
        copy.start()

    def line(x, y):
        x, y = (x + 4) % 4, (y + 4) % 4
        rr, base = (x // 2) * 4 + y, (x % 2) * 8
        return rr * 2 + core, base, rr * 16 + base

    chip = line(x, y)[2] + z
    ring = [(z + d) % 8 for d in range(8)]
    outward = (4, 3, 5, 2, 6, 1, 7, 0)

    barrier = pltpu.get_barrier_semaphore()
    for dx in (2, 1, 3):
        to_row, base, _ = line(x + dx, y)
        pl.semaphore_signal(barrier, inc=1, device_id=(to_row, base + z), device_id_type=MESH)
    for dy in (2, 1, 3, 0):
        to_row, base, _ = line(x, y + dy)
        for dz in outward[: 8 if dy else 7]:
            pl.semaphore_signal(
                barrier, inc=1, device_id=(to_row, base + ring[dz]), device_id_type=MESH
            )
    pl.semaphore_signal(barrier, inc=1, device_id=other, device_id_type=MESH)

    for copy in inputs:
        copy.wait()

    lane = lax.broadcasted_iota(jnp.int32, (8, 128), 1)
    first = lax.broadcasted_iota(jnp.int32, (8, 128), 0) + 8 * (lane // 32)
    row_mask = jnp.zeros((8, 128), jnp.int32)
    col_mask = jnp.zeros((8, 128), jnp.int32)
    for a in range(32):
        row_mask = jnp.where(first == a, mask_ref[row * 32 + a], row_mask)
        col_mask = jnp.where(lane % 32 == a, mask_ref[col * 32 + a], col_mask)
    token_mask = row_mask.astype(F32) * col_mask.astype(F32)

    def prepare(u):
        for k in range(2):
            wt[u, pl.ds(128 * k, 128)] = pw_ref[u, :, pl.ds(128 * k, 128)].T
            wt[u, pl.ds(256 + 128 * k, 128)] = gw_ref[u, :, pl.ds(128 * k, 128)].T
        wt[u, pl.ds(512, 128)] = ow_ref[u].T
        ft[u] = fw_ref[u].T
        for k, ref in enumerate((ng_ref, nb_ref, og_ref, ob_ref)):
            gb[4 * u + k] = jnp.broadcast_to(ref[pl.ds(u, 1), :], (128, 128)).T

    def project(u, s, z_s):
        normed = normalize(z_s, gb[4 * u], gb[4 * u + 1]).astype(BF16)
        product = dot(wt[u], normed, ((1,), (0,)))
        close[s] = sigmoid(product[512:])
        half[pl.ds(s, 256, stride=8), :] = (
            sigmoid(product[256:512]) * product[:256] * token_mask[s : s + 1]
        )

    def pack(u, side, p):
        rows = pl.multiple_of(p * 8, 64)
        fsend[u, side, pl.ds(p, 8)] = (
            half[pl.ds(rows + 1024 * side, 64), :].reshape(8, 8, 128).astype(BF16)
        )

    def send_tile(src, dst, send_sem, recv_sem, device, here):
        def send():
            pltpu.make_async_remote_copy(
                src, dst, send_sem, recv_sem, device_id=device, device_id_type=MESH
            ).start()

        if here is False:
            send()
        else:
            pl.when(jnp.logical_not(here))(send)

            @pl.when(here)
            def _():
                pltpu.make_async_copy(src, dst, recv_sem).start()

    def send_right(u, dx, dy, m):
        to_row, base, p = line(x + dx, y + dy)
        pack(u, 1, p)
        for dz in outward:
            to = p + ring[dz]
            send_tile(
                fsend.at[u, 1, to], frecv.at[u, chip], f_send.at[u], f_recv.at[u, m],
                (to_row, base + ring[dz]), False if dz else to == chip,
            )

    def whole(src, dst, send, recv):
        return pltpu.make_async_remote_copy(
            src, dst, send, recv, device_id=other, device_id_type=MESH
        )

    def arrange(tiles):
        return jnp.concatenate(chunk_swap([v.astype(F32) for v in tiles]), axis=0).astype(BF16)

    def arrange_right(u, dx, dy, m):
        p = line(x - dx, y - dy)[2]
        part = frecv.at[u, pl.ds(p, 8)]
        whole(part, part, f_send.at[u], f_recv.at[u, m]).wait_recv()
        rr, g = p // 16, (p // 8) % 2
        rows = pl.ds(pl.multiple_of(rr * 32, 32), 32)
        lanes = pl.ds(pl.multiple_of(g * 128, 128), 128)
        for t in range(2):
            right[u, t, rows, lanes] = arrange([frecv[u, p + 2 * k + t] for k in range(4)])
        whole(
            right.at[u, :, rows, lanes], right_in.at[u, :, rows, lanes], x_send.at[u], x_recv.at[u]
        ).start()

    def send_rows(u, parts):
        for rr, first_row in parts:
            for t in range(2):
                for g in range(2):
                    tiles = [
                        sums[t, pl.ds(first_row + 8 * k, 8), pl.ds(128 * g, 128)] for k in range(4)
                    ]
                    for k, tile in enumerate(chunk_swap(tiles)):
                        bsend[u, rr * 16 + 8 * g + 2 * k + t] = tile.astype(BF16)
        for rr, _ in parts:
            for d in (1, 0):
                base = ((col // 8 + d) % 2) * 8
                for dz in outward:
                    to = rr * 16 + base + ring[dz]
                    send_tile(
                        bsend.at[u, to], brecv.at[u, chip], b_send.at[u], b_recv.at[u],
                        (rr * 2 + core, base + ring[dz]), False if d or dz else to == chip,
                    )

    def receive_sums(u):
        whole(bsend.at[u], brecv.at[u], b_send.at[u], b_recv.at[u]).wait_recv()
        wide[...] = brecv[u].astype(F32).reshape(1024, 128)

    def finish(u, s):
        summed = wide[pl.ds(s, 128, stride=8), :]
        lifted = normalize(summed, gb[4 * u + 2], gb[4 * u + 3]).astype(BF16)
        update = close[s] * dot(ft[u], lifted, ((1,), (0,)))
        return (zt[s].astype(F32) + update).astype(BF16)

    prepare(0)
    for s in range(8):
        z_s = jnp.concatenate([x_ref[8 * k + s] for k in range(4)], axis=0).T
        zt[s] = z_s
        project(0, s, z_s.astype(F32))

    pl.semaphore_wait(barrier, 35)
    for dx in (2, 1, 3):
        to_row, base, _ = line(x + dx, y)
        pl.semaphore_signal(
            entry.at[dx], inc=1, device_id=(to_row, base + z), device_id_type=MESH
        )

    def outer(n):
        return (1 + 2 * (n // 4)) % 5 + 2 * (n // 8), far_first(n % 4), 4 + n

    @pl.loop(0, 4)
    def _(n):
        send_right(0, 0, far_first(n), n)

    for k, dx in enumerate((1, 3, 2)):
        pl.semaphore_wait(entry.at[4 - dx], 1)

        @pl.loop(0, 4)
        def _(n):
            send_right(0, dx, far_first(n), 4 + 4 * k + n)

    def part_of(n):
        return (x // 2 + 1 - n // 4) % 2, far_first(n % 4)

    @pl.loop(0, 8)
    def _(n):
        x_hi, dy = part_of(n)
        for d in (1, 0):
            to_row, base, p = line(2 * x_hi + (x + d) % 2, y + dy)
            pack(0, 0, p)
            for dz in outward:
                to = p + ring[dz]
                send_tile(
                    fsend.at[0, 0, to], lrecv.at[chip], l_send.at[0], l_recv.at[n],
                    (to_row, base + ring[dz]), False if d or dz else to == chip,
                )

    prepare(1)

    @pl.loop(0, 4)
    def _(n):
        arrange_right(0, 0, far_first(n), n)

    @pl.loop(0, 12)
    def _(n):
        arrange_right(0, *outer(n))

    swap = whole(right.at[0], right_in.at[0], x_send.at[0], x_recv.at[0])
    for t in range(2):
        turned[core, t] = right[0, t].T
    swap.wait_recv()
    for t in range(2):
        turned[1 - core, t] = right_in[0, t].T

    @pl.loop(0, 4)
    def _(n):
        parts, rows = [], ([], [])
        for half_of in range(2):
            x_hi, dy = part_of(2 * n + half_of)
            rr = x_hi * 4 + (y + 4 - dy) % 4
            part = lrecv.at[pl.ds(rr * 16, 16)]
            whole(part, part, l_send.at[0], l_recv.at[2 * n + half_of]).wait_recv()
            parts.append((rr, 32 * half_of))
        for rr, _ in parts:
            for t in range(2):
                tiles = [
                    arrange([lrecv[rr * 16 + 8 * g + 2 * k + t] for k in range(4)]) for g in range(2)
                ]
                rows[t].append(jnp.concatenate(tiles, axis=1))
        rows = [jnp.concatenate(v, axis=0) for v in rows]
        for t in range(2):
            sums[t, pl.ds(0, 64)] = dot(rows[0], turned[t, 0], ((1,), (0,))) + dot(
                rows[1], turned[t, 1], ((1,), (0,))
            )
        send_rows(0, parts)

    receive_sums(0)

    for s in range(8):
        z_s = finish(0, s)
        zt[s] = z_s
        project(1, s, z_s.astype(F32))

    def nth(n):
        return far_first(n // 4), far_first(n % 4), n

    @pl.loop(0, 16)
    def _(n):
        send_right(1, *nth(n))

    summing = z % 2

    @pl.loop(0, 2)
    def _(n):
        x_lo = (x + 1 + n) % 2

        @pl.loop(0, 8)
        def _(k):
            x_hi = (x // 2 + 1 + k % 2) % 2
            to_row, base, p = line(2 * x_hi + x_lo, y + far_first(k // 2))
            to_row = to_row - core + summing
            pack(1, 0, p)
            for dz in outward:
                to = p + ring[dz]
                here = jnp.logical_and(to == chip, summing == core)
                send_tile(
                    fsend.at[1, 0, to], lrecv_1.at[core, chip], l_send.at[1], l_recv_1.at[n],
                    (to_row, base + ring[dz]), False if dz else here,
                )

    @pl.loop(0, 16)
    def _(n):
        arrange_right(1, *nth(n))

    swap_1 = whole(right.at[1], right_in.at[1], x_send.at[1], x_recv.at[1])
    swap_1.wait_recv()

    @pl.loop(0, 2)
    def _(n):
        g = (x + 1 + n) % 2
        part = lrecv_1.at[0, pl.ds(0, 64)]
        whole(part, part, l_send.at[1], l_recv_1.at[n]).wait_recv()

        @pl.loop(0, 2)
        def _(quarter):
            for k in range(4):
                rr = 4 * quarter + k
                rows = pl.ds(pl.multiple_of(rr * 32, 32), 32)
                for c in range(2):
                    left[c, rows, :] = arrange(
                        [lrecv_1[c, rr * 16 + 8 * g + 2 * m + core] for m in range(4)]
                    )

        for t in range(2):
            sums[t] = dot(left[core], right[1, t], ((0,), (0,))) + dot(
                left[1 - core], right_in[1, t], ((0,), (0,))
            )

        @pl.loop(0, 2)
        def _(k):
            parts = []
            for m in range(2):
                to_y = (y + far_first(2 * k + m)) % 4
                parts.append((g * 4 + to_y, pl.multiple_of(to_y * 32, 32)))
            send_rows(1, parts)

    receive_sums(1)

    for s in range(8):
        z_s = finish(1, s).T
        for k in range(4):
            out_ref[8 * k + s] = z_s[32 * k : 32 * k + 32]

    swap.wait_send()
    swap_1.wait_send()
    most = pl.ds(0, 127)
    for u in range(2):
        for side, send in ((1, f_send), (0, l_send)):
            sent = fsend.at[u, side, most]
            whole(sent, sent, send.at[u], f_recv.at[u, 0]).wait_send()
        whole(bsend.at[u, most], brecv.at[u, most], b_send.at[u], b_recv.at[u]).wait_send()

    @pl.when(summing != core)
    def _():
        sent = fsend.at[1, 0, 0]
        whole(sent, sent, l_send.at[1], f_recv.at[1, 0]).wait_send()


def shards(*arrays):
    vmem = pl.BlockSpec(memory_space=pltpu.VMEM)
    hbm = pl.BlockSpec(memory_space=pltpu.HBM)
    return pl.pallas_call(
        kernel,
        out_shape=jax.ShapeDtypeStruct(arrays[0].shape, BF16),
        in_specs=[hbm] * 10,
        out_specs=vmem,
        scratch_shapes=[
            (pltpu.SMEM if array.ndim == 1 else pltpu.VMEM)(array.shape, array.dtype)
            for array in arrays
        ]
        + [
            pltpu.VMEM((2, 640, 128), BF16),
            pltpu.VMEM((2, 128, 128), BF16),
            pltpu.VMEM((8, 128, 128), F32),
            pltpu.VMEM((8, 128, 128), BF16),
            pltpu.VMEM((8, 128, 128), F32),
            pltpu.VMEM((2048, 128), F32),
            pltpu.VMEM((2, 2, 128, 8, 128), BF16),
            pltpu.VMEM((2, 128, 8, 128), BF16),
            pltpu.VMEM((128, 8, 128), BF16),
            pltpu.VMEM((2, 128, 8, 128), BF16),
            pltpu.VMEM((2, 256, 128), BF16),
            pltpu.VMEM((2, 2, 256, 256), BF16),
            pltpu.VMEM((2, 2, 256, 256), BF16),
            pltpu.VMEM((2, 2, 256, 256), BF16),
            pltpu.VMEM((2, 128, 256), F32),
            pltpu.VMEM((2, 128, 8, 128), BF16),
            pltpu.VMEM((2, 128, 8, 128), BF16),
            pltpu.VMEM((1024, 128), F32),
            pltpu.SemaphoreType.DMA((10,)),
            pltpu.SemaphoreType.REGULAR((4,)),
            pltpu.SemaphoreType.DMA((2,)),
            pltpu.SemaphoreType.DMA((2, 16)),
            pltpu.SemaphoreType.DMA((2,)),
            pltpu.SemaphoreType.DMA((8,)),
            pltpu.SemaphoreType.DMA((2,)),
            pltpu.SemaphoreType.DMA((2,)),
            pltpu.SemaphoreType.DMA((2,)),
            pltpu.SemaphoreType.DMA((2,)),
            pltpu.SemaphoreType.DMA((2,)),
        ],
        compiler_params=pltpu.CompilerParams(
            collective_id=0, has_side_effects=True, vmem_limit_bytes=32 << 20
        ),
    )(*(pltpu.with_memory_space_constraint(array, pltpu.HBM) for array in arrays))


def solution(mesh):
    return jax.shard_map(
        shards,
        mesh=mesh,
        in_specs=(P("row", "col", None), P(), P(), P(), P(), P(), P(), P(), P(), P()),
        out_specs=P("row", "col", None),
        check_vma=False,
    )
```

```python
import jax
import jax.numpy as jnp
from jax import lax
from jax.experimental import pallas as pl
from jax.experimental.pallas import tpu as pltpu
from jax.sharding import PartitionSpec as P

MESH = pl.DeviceIdType.MESH
F32 = jnp.float32
BF16 = jnp.bfloat16


def far_first(n):
    return n + 2 - (n // 2) * (2 * n - 1)


def dot(a, b, dims):
    return lax.dot_general(a, b, (dims, ((), ())), preferred_element_type=F32)


def sigmoid(v):
    return 0.5 * jnp.tanh(0.5 * v) + 0.5


def normalize(v, gain, bias):
    average = jnp.mean(v, axis=0, keepdims=True)
    centred = v - average
    variance = jnp.mean(centred * centred, axis=0, keepdims=True)
    return centred * lax.rsqrt(variance + 1e-05) * gain + bias


def chunk_swap(v):
    lane = lax.broadcasted_iota(jnp.int32, v[0].shape, 1)
    odd = (lane // 32) % 2 == 1
    high = lane >= 64

    def pair(a, b, shift, mask):
        return jnp.where(mask, pltpu.roll(b, shift, 1), a), jnp.where(
            mask, b, pltpu.roll(a, 128 - shift, 1)
        )

    a, b = pair(v[0], v[1], 32, odd)
    c, d = pair(v[2], v[3], 32, odd)
    a, c = pair(a, c, 64, high)
    b, d = pair(b, d, 64, high)
    return a, b, c, d


def kernel(
    x_hbm, mask_hbm, ng_hbm, nb_hbm, pw_hbm, gw_hbm, og_hbm, ob_hbm, fw_hbm, ow_hbm,
    out_ref,
    x_ref, mask_ref, ng_ref, nb_ref, pw_ref, gw_ref, og_ref, ob_ref, fw_ref, ow_ref,
    wt, ft, gb, zt, normed, close, half, fsend, frecv, lrecv, lrecv_1, left, right, right_in, turned, sums, bsend, brecv, wide,
    in_sem, entry, f_send, f_recv, l_send, l_recv, l_recv_1, b_send, b_recv, x_send, x_recv,
):
    row, col = lax.axis_index("row"), lax.axis_index("col")
    core = row % 2
    x, y, z = (row // 8) * 2 + col // 8, (row // 2) % 4, col % 8
    other = (row + 1 - 2 * core, col)

    hbm = (x_hbm, mask_hbm, ng_hbm, nb_hbm, pw_hbm, gw_hbm, og_hbm, ob_hbm, fw_hbm, ow_hbm)
    held = (x_ref, mask_ref, ng_ref, nb_ref, pw_ref, gw_ref, og_ref, ob_ref, fw_ref, ow_ref)
    inputs = [
        pltpu.make_async_copy(a, b, in_sem.at[k]) for k, (a, b) in enumerate(zip(hbm, held))
    ]
    for copy in inputs:
        copy.start()

    def line(x, y):
        x, y = (x + 4) % 4, (y + 4) % 4
        rr, base = (x // 2) * 4 + y, (x % 2) * 8
        return rr * 2 + core, base, rr * 16 + base

    chip = line(x, y)[2] + z
    ring = [(z + d) % 8 for d in range(8)]
    outward = (4, 3, 5, 2, 6, 1, 7, 0)

    barrier = pltpu.get_barrier_semaphore()
    for dx in (2, 1, 3):
        to_row, base, _ = line(x + dx, y)
        pl.semaphore_signal(barrier, inc=1, device_id=(to_row, base + z), device_id_type=MESH)
    for dy in (2, 1, 3, 0):
        to_row, base, _ = line(x, y + dy)
        for dz in outward[: 8 if dy else 7]:
            pl.semaphore_signal(
                barrier, inc=1, device_id=(to_row, base + ring[dz]), device_id_type=MESH
            )
    pl.semaphore_signal(barrier, inc=1, device_id=other, device_id_type=MESH)

    for copy in inputs:
        copy.wait()

    lane = lax.broadcasted_iota(jnp.int32, (8, 128), 1)
    first = lax.broadcasted_iota(jnp.int32, (8, 128), 0) + 8 * (lane // 32)
    row_mask = jnp.zeros((8, 128), jnp.int32)
    col_mask = jnp.zeros((8, 128), jnp.int32)
    for a in range(32):
        row_mask = jnp.where(first == a, mask_ref[row * 32 + a], row_mask)
        col_mask = jnp.where(lane % 32 == a, mask_ref[col * 32 + a], col_mask)
    token_mask = row_mask.astype(F32) * col_mask.astype(F32)

    def prepare(u):
        for k in range(2):
            side = pl.ds(128 - 128 * k, 128)
            wt[u, pl.ds(256 * k, 128)] = pw_ref[u, :, side].T
            wt[u, pl.ds(256 * k + 128, 128)] = gw_ref[u, :, side].T
        wt[u, pl.ds(512, 128)] = ow_ref[u].T
        ft[u] = fw_ref[u].T
        for k, ref in enumerate((ng_ref, nb_ref, og_ref, ob_ref)):
            gb[4 * u + k] = jnp.broadcast_to(ref[pl.ds(u, 1), :], (128, 128)).T

    def project_right(u, s, z_s):
        normed[s] = normalize(z_s, gb[4 * u], gb[4 * u + 1]).astype(BF16)
        product = dot(wt[u, pl.ds(0, 256)], normed[s], ((1,), (0,)))
        half[pl.ds(1024 + s, 128, stride=8), :] = (
            sigmoid(product[128:]) * product[:128] * token_mask[s : s + 1]
        )

    def project_left(u):
        for s in range(8):
            product = dot(wt[u, pl.ds(256, 384)], normed[s], ((1,), (0,)))
            half[pl.ds(s, 128, stride=8), :] = (
                sigmoid(product[128:256]) * product[:128] * token_mask[s : s + 1]
            )
            close[s] = sigmoid(product[256:])

    def pack(u, side, p):
        rows = pl.multiple_of(p * 8, 64)
        fsend[u, side, pl.ds(p, 8)] = (
            half[pl.ds(rows + 1024 * side, 64), :].reshape(8, 8, 128).astype(BF16)
        )

    def send_tile(src, dst, send_sem, recv_sem, device, here):
        def send():
            pltpu.make_async_remote_copy(
                src, dst, send_sem, recv_sem, device_id=device, device_id_type=MESH
            ).start()

        if here is False:
            send()
        else:
            pl.when(jnp.logical_not(here))(send)

            @pl.when(here)
            def _():
                pltpu.make_async_copy(src, dst, recv_sem).start()

    def send_right(u, dx, dy, m):
        to_row, base, p = line(x + dx, y + dy)
        pack(u, 1, p)
        for dz in outward:
            to = p + ring[dz]
            send_tile(
                fsend.at[u, 1, to], frecv.at[u, chip], f_send.at[u], f_recv.at[u, m],
                (to_row, base + ring[dz]), False if dz else to == chip,
            )

    def whole(src, dst, send, recv):
        return pltpu.make_async_remote_copy(
            src, dst, send, recv, device_id=other, device_id_type=MESH
        )

    def arrange(tiles):
        return jnp.concatenate(chunk_swap([v.astype(F32) for v in tiles]), axis=0).astype(BF16)

    def arrange_right(u, dx, dy, m):
        p = line(x - dx, y - dy)[2]
        part = frecv.at[u, pl.ds(p, 8)]
        whole(part, part, f_send.at[u], f_recv.at[u, m]).wait_recv()
        rr, g = p // 16, (p // 8) % 2
        rows = pl.ds(pl.multiple_of(rr * 32, 32), 32)
        lanes = pl.ds(pl.multiple_of(g * 128, 128), 128)
        for t in range(2):
            right[u, t, rows, lanes] = arrange([frecv[u, p + 2 * k + t] for k in range(4)])
        whole(
            right.at[u, :, rows, lanes], right_in.at[u, :, rows, lanes], x_send.at[u], x_recv.at[u]
        ).start()

    def send_rows(u, parts):
        for rr, first_row in parts:
            for t in range(2):
                for g in range(2):
                    tiles = [
                        sums[t, pl.ds(first_row + 8 * k, 8), pl.ds(128 * g, 128)] for k in range(4)
                    ]
                    for k, tile in enumerate(chunk_swap(tiles)):
                        bsend[u, rr * 16 + 8 * g + 2 * k + t] = tile.astype(BF16)
        for rr, _ in parts:
            for d in (1, 0):
                base = ((x + d + x // 2 + rr // 4) % 2) * 8
                for dz in outward:
                    to = rr * 16 + base + ring[dz]
                    send_tile(
                        bsend.at[u, to], brecv.at[u, chip], b_send.at[u], b_recv.at[u],
                        (rr * 2 + core, base + ring[dz]), False if d or dz else to == chip,
                    )

    def receive_sums(u):
        whole(bsend.at[u], brecv.at[u], b_send.at[u], b_recv.at[u]).wait_recv()
        wide[...] = brecv[u].astype(F32).reshape(1024, 128)

    def finish(u, s):
        summed = wide[pl.ds(s, 128, stride=8), :]
        lifted = normalize(summed, gb[4 * u + 2], gb[4 * u + 3]).astype(BF16)
        update = close[s] * dot(ft[u], lifted, ((1,), (0,)))
        return (zt[s].astype(F32) + update).astype(BF16)

    prepare(0)
    for s in range(8):
        z_s = jnp.concatenate([x_ref[8 * k + s] for k in range(4)], axis=0).T
        zt[s] = z_s
        project_right(0, s, z_s.astype(F32))

    pl.semaphore_wait(barrier, 35)
    for dx in (2, 1, 3):
        to_row, base, _ = line(x + dx, y)
        pl.semaphore_signal(
            entry.at[dx], inc=1, device_id=(to_row, base + z), device_id_type=MESH
        )

    def outer(n):
        return (1 + 2 * (n // 4)) % 5 + 2 * (n // 8), far_first(n % 4), 4 + n

    @pl.loop(0, 4)
    def _(n):
        send_right(0, 0, far_first(n), n)

    project_left(0)
    for k, dx in enumerate((1, 3, 2)):
        pl.semaphore_wait(entry.at[4 - dx], 1)

        @pl.loop(0, 4)
        def _(n):
            send_right(0, dx, far_first(n), 4 + 4 * k + n)

    def part_of(n):
        return (x // 2 + 1 - n // 4) % 2, far_first(n % 4)

    @pl.loop(0, 8)
    def _(n):
        x_hi, dy = part_of(n)
        for d in (1, 0):
            to_row, base, p = line(2 * x_hi + (x + d + 1 - n // 4) % 2, y + dy)
            pack(0, 0, p)
            for dz in outward:
                to = p + ring[dz]
                send_tile(
                    fsend.at[0, 0, to], lrecv.at[chip], l_send.at[0], l_recv.at[n],
                    (to_row, base + ring[dz]), False if d or dz else to == chip,
                )

    prepare(1)

    @pl.loop(0, 4)
    def _(n):
        arrange_right(0, 0, far_first(n), n)

    @pl.loop(0, 12)
    def _(n):
        arrange_right(0, *outer(n))

    swap = whole(right.at[0], right_in.at[0], x_send.at[0], x_recv.at[0])
    for t in range(2):
        turned[core, t] = right[0, t].T
    swap.wait_recv()
    for t in range(2):
        turned[1 - core, t] = right_in[0, t].T

    @pl.loop(0, 4)
    def _(n):
        parts, rows = [], ([], [])
        for half_of in range(2):
            x_hi, dy = part_of(2 * n + half_of)
            rr = x_hi * 4 + (y + 4 - dy) % 4
            part = lrecv.at[pl.ds(rr * 16, 16)]
            whole(part, part, l_send.at[0], l_recv.at[2 * n + half_of]).wait_recv()
            parts.append((rr, 32 * half_of))
        for rr, _ in parts:
            for t in range(2):
                tiles = [
                    arrange([lrecv[rr * 16 + 8 * g + 2 * k + t] for k in range(4)]) for g in range(2)
                ]
                rows[t].append(jnp.concatenate(tiles, axis=1))
        rows = [jnp.concatenate(v, axis=0) for v in rows]
        for t in range(2):
            sums[t, pl.ds(0, 64)] = dot(rows[0], turned[t, 0], ((1,), (0,))) + dot(
                rows[1], turned[t, 1], ((1,), (0,))
            )
        send_rows(0, parts)

    receive_sums(0)

    for s in range(8):
        z_s = finish(0, s)
        zt[s] = z_s
        project_right(1, s, z_s.astype(F32))

    def nth(n):
        return far_first(n // 4), far_first(n % 4), n

    @pl.loop(0, 16)
    def _(n):
        send_right(1, *nth(n))

    project_left(1)

    summing = z % 2

    @pl.loop(0, 2)
    def _(n):
        x_lo = (x + 1 + n) % 2

        @pl.loop(0, 8)
        def _(k):
            x_hi = (x // 2 + 1 + k % 2) % 2
            to_row, base, p = line(2 * x_hi + x_lo, y + far_first(k // 2))
            to_row = to_row - core + summing
            pack(1, 0, p)
            for dz in outward:
                to = p + ring[dz]
                here = jnp.logical_and(to == chip, summing == core)
                send_tile(
                    fsend.at[1, 0, to], lrecv_1.at[core, chip], l_send.at[1], l_recv_1.at[n],
                    (to_row, base + ring[dz]), False if dz else here,
                )

    @pl.loop(0, 16)
    def _(n):
        arrange_right(1, *nth(n))

    swap_1 = whole(right.at[1], right_in.at[1], x_send.at[1], x_recv.at[1])
    swap_1.wait_recv()

    @pl.loop(0, 2)
    def _(n):
        g = (x + 1 + n) % 2
        part = lrecv_1.at[0, pl.ds(0, 64)]
        whole(part, part, l_send.at[1], l_recv_1.at[n]).wait_recv()

        @pl.loop(0, 2)
        def _(quarter):
            for k in range(4):
                rr = 4 * quarter + k
                rows = pl.ds(pl.multiple_of(rr * 32, 32), 32)
                for c in range(2):
                    left[c, rows, :] = arrange(
                        [lrecv_1[c, rr * 16 + 8 * g + 2 * m + core] for m in range(4)]
                    )

        for t in range(2):
            sums[t] = dot(left[core], right[1, t], ((0,), (0,))) + dot(
                left[1 - core], right_in[1, t], ((0,), (0,))
            )

        @pl.loop(0, 2)
        def _(k):
            parts = []
            for m in range(2):
                to_y = (y + far_first(2 * k + m)) % 4
                parts.append((g * 4 + to_y, pl.multiple_of(to_y * 32, 32)))
            send_rows(1, parts)

    receive_sums(1)

    for s in range(8):
        z_s = finish(1, s).T
        for k in range(4):
            out_ref[8 * k + s] = z_s[32 * k : 32 * k + 32]

    swap.wait_send()
    swap_1.wait_send()
    most = pl.ds(0, 127)
    for u in range(2):
        for side, send in ((1, f_send), (0, l_send)):
            sent = fsend.at[u, side, most]
            whole(sent, sent, send.at[u], f_recv.at[u, 0]).wait_send()
        whole(bsend.at[u, most], brecv.at[u, most], b_send.at[u], b_recv.at[u]).wait_send()

    @pl.when(summing != core)
    def _():
        sent = fsend.at[1, 0, 0]
        whole(sent, sent, l_send.at[1], f_recv.at[1, 0]).wait_send()


def shards(*arrays):
    vmem = pl.BlockSpec(memory_space=pltpu.VMEM)
    hbm = pl.BlockSpec(memory_space=pltpu.HBM)
    return pl.pallas_call(
        kernel,
        out_shape=jax.ShapeDtypeStruct(arrays[0].shape, BF16),
        in_specs=[hbm] * 10,
        out_specs=vmem,
        scratch_shapes=[
            (pltpu.SMEM if array.ndim == 1 else pltpu.VMEM)(array.shape, array.dtype)
            for array in arrays
        ]
        + [
            pltpu.VMEM((2, 640, 128), BF16),
            pltpu.VMEM((2, 128, 128), BF16),
            pltpu.VMEM((8, 128, 128), F32),
            pltpu.VMEM((8, 128, 128), BF16),
            pltpu.VMEM((8, 128, 128), BF16),
            pltpu.VMEM((8, 128, 128), F32),
            pltpu.VMEM((2048, 128), F32),
            pltpu.VMEM((2, 2, 128, 8, 128), BF16),
            pltpu.VMEM((2, 128, 8, 128), BF16),
            pltpu.VMEM((128, 8, 128), BF16),
            pltpu.VMEM((2, 128, 8, 128), BF16),
            pltpu.VMEM((2, 256, 128), BF16),
            pltpu.VMEM((2, 2, 256, 256), BF16),
            pltpu.VMEM((2, 2, 256, 256), BF16),
            pltpu.VMEM((2, 2, 256, 256), BF16),
            pltpu.VMEM((2, 128, 256), F32),
            pltpu.VMEM((2, 128, 8, 128), BF16),
            pltpu.VMEM((2, 128, 8, 128), BF16),
            pltpu.VMEM((1024, 128), F32),
            pltpu.SemaphoreType.DMA((10,)),
            pltpu.SemaphoreType.REGULAR((4,)),
            pltpu.SemaphoreType.DMA((2,)),
            pltpu.SemaphoreType.DMA((2, 16)),
            pltpu.SemaphoreType.DMA((2,)),
            pltpu.SemaphoreType.DMA((8,)),
            pltpu.SemaphoreType.DMA((2,)),
            pltpu.SemaphoreType.DMA((2,)),
            pltpu.SemaphoreType.DMA((2,)),
            pltpu.SemaphoreType.DMA((2,)),
            pltpu.SemaphoreType.DMA((2,)),
        ],
        compiler_params=pltpu.CompilerParams(
            collective_id=0, has_side_effects=True, vmem_limit_bytes=32 << 20
        ),
    )(*(pltpu.with_memory_space_constraint(array, pltpu.HBM) for array in arrays))


def solution(mesh):
    return jax.shard_map(
        shards,
        mesh=mesh,
        in_specs=(P("row", "col", None), P(), P(), P(), P(), P(), P(), P(), P(), P()),
        out_specs=P("row", "col", None),
        check_vma=False,
    )
```
